512 devices in a mesh: lat: 64 (over z_lo, y, x), chan: 8 (over z_hi, core).
Axes of the slice: x: 4, y: 4, z: 16 (z_hi: 4, z_lo: 4; z = z_hi * 4 + z_lo), core: 2. Of those that a mesh axis runs over, the one named last changes fastest.
Arguments:
- ocean_state: bfloat16 [384, 256, 1440], P('lat', 'chan'), may hold values from -6 to 6
- land_mask: int32 [384, 1440], P('lat', 'chan'), may hold values 0 or 1
- order_table: int32 [384], replicated, may hold values from 0 to 383, each once
- spectral_weight: bfloat16 [384, 2, 256, 256], P('lat', None, 'chan'), may hold values from -0.25 to 0.25
- inner_weight: bfloat16 [256, 512], P(None, 'chan'), may hold values from -0.375 to 0.375
- outer_weight: bfloat16 [512, 256], P('chan'), may hold values from -0.25 to 0.25
Outputs:
- layer_output: bfloat16 [384, 1440, 256], P('lat', 'chan')
The draws below stay inside these ranges and needn't reach their ends.
Inputs may be any that keep to these rules, and one draw needn't show every extreme that they name: `order_table`: a permutation: every order from 0 to 383 stands in exactly one slot.
All inputs are finite; a program needn't handle non-finite values. Where the reference program divides by a largest or mean magnitude, that divisor is 1e-20 or more. No bound on the sum of `land_mask` on one device may be relied on, other than what follows from the above.
Results may differ from the reference program's by a relative error of at most 0.0095.
Values may be sent and summed in bfloat16 or wider, within the bound.
A program may use at most 64 MiB of HBM per device.

```python
import math
import jax
import jax.numpy as jnp
from jax import lax

NLAT = 384
NLON = 1440
MODES = 384
CHANNELS = 256
FFN = 512


def plant(drawn, own_key, smallest, high):
    longest = drawn.shape.index(max(drawn.shape))
    spots = []
    for shift in (0, 1):
        where = [jax.random.randint(jax.random.fold_in(own_key, axis), (), 0, length) for axis, length in enumerate(drawn.shape)]
        where[longest] = (where[longest] + shift) % drawn.shape[longest]
        spots.append(tuple(where))
    return drawn.at[spots[0]].set(smallest).at[spots[1]].set(high)


def level_of(key, dims, shards, least, top_value):
    factor_of = 1.0
    for dim, blocks in shards:
        heights = jax.random.uniform(jax.random.fold_in(jax.random.fold_in(key, 6), dim), (blocks,), jnp.float32, least / len(shards), top_value / len(shards))
        factor_of = factor_of * jnp.repeat(jnp.exp(heights), dims[dim] // blocks).reshape((-1,) + (1,) * (len(dims) - 1 - dim))
    return factor_of


def bell_draw(rng, extent, scale, reach, split=(), kind=jnp.bfloat16):
    values = scale * jax.random.normal(rng, extent, jnp.float32)
    if split:
        values = values * level_of(rng, extent, split, -0.22, 0.18)
    return jnp.clip(values, -reach, reach).astype(kind)


def setup_inputs(seed: int = 0) -> dict:
    splits = jax.random.split(jax.random.key(seed), 7)
    ocean_state = bell_draw(splits[0], (NLAT, CHANNELS, NLON), 1.0, 6.0, ((0, 64), (1, 8)))
    land_mask = plant((jax.random.randint(splits[1], (NLAT, NLON), 0, 10) < 7).astype(jnp.int32), jax.random.fold_in(splits[1], 1), 0, 1)
    order_table = jax.random.permutation(splits[2], MODES).astype(jnp.int32)
    spectral_weight = bell_draw(splits[3], (MODES, 2, CHANNELS, CHANNELS), (2 * CHANNELS) ** -0.5, 0.25, ((0, 64), (2, 8)))
    inner_weight = bell_draw(splits[4], (CHANNELS, FFN), CHANNELS ** -0.5, 0.375, ((1, 8),))
    outer_weight = bell_draw(splits[5], (FFN, CHANNELS), FFN ** -0.5, 0.25, ((0, 8),))
    return {"ocean_state": ocean_state, "land_mask": land_mask, "order_table": order_table, "spectral_weight": spectral_weight, "inner_weight": inner_weight, "outer_weight": outer_weight}


def fejer_weights():
    colatitude = (jnp.arange(NLAT, dtype=jnp.float32) + 0.5) * (math.pi / NLAT)
    harmonic = jnp.arange(1, NLAT // 2 + 1).astype(jnp.float32)
    series = jnp.cos(2.0 * colatitude[:, None] * harmonic[None, :]) / (4.0 * harmonic * harmonic - 1.0)[None, :]
    return 2.0 / NLAT * (1.0 - 2.0 * lax.optimization_barrier(jnp.sum(series, axis=1)))

def compose(earlier, latter):
    first_mat, first_log = earlier
    second_mat, second_log = latter
    product = jnp.stack([second_mat[0] * first_mat[0] + second_mat[1] * first_mat[2], second_mat[0] * first_mat[1] + second_mat[1] * first_mat[3], second_mat[2] * first_mat[0] + second_mat[3] * first_mat[2], second_mat[2] * first_mat[1] + second_mat[3] * first_mat[3]])
    largest = lax.optimization_barrier(jnp.max(jnp.abs(product), axis=0, keepdims=True))
    return (product / largest, first_log + second_log + jnp.log(largest))

def legendre_rows(order_value):
    half_rows = NLAT // 2
    colatitude = (jnp.arange(half_rows, dtype=jnp.float32) + 0.5) * (math.pi / NLAT)
    cosine = jnp.cos(colatitude)
    sine_part = jnp.sin(colatitude)
    offsets = jnp.arange(MODES).astype(jnp.float32)
    order_float = order_value.astype(jnp.float32)
    degree = order_float + offsets
    beyond_start = offsets >= 1.0
    denominator = jnp.where(beyond_start, degree * degree - order_float * order_float, 1.0)
    upper_coef = jnp.sqrt((4.0 * degree * degree - 1.0) / denominator)
    previous = degree - 1.0
    lower_coef = jnp.sqrt(jnp.maximum(previous * previous - order_float * order_float, 0.0) / jnp.maximum(4.0 * previous * previous - 1.0, 1.0))
    filled = jnp.ones((MODES, half_rows), jnp.float32)
    beyond_column = beyond_start[:, None]
    matrix = jnp.stack([jnp.where(beyond_column, upper_coef[:, None] * cosine[None, :], filled), jnp.where(beyond_column, -(upper_coef * lower_coef)[:, None] * filled, 0.0 * filled), jnp.where(beyond_column, filled, 0.0 * filled), jnp.where(beyond_column, 0.0 * filled, filled)])
    log_scale = jnp.zeros((1, MODES, half_rows), jnp.float32)
    matrix, log_scale = lax.associative_scan(compose, (matrix, log_scale), axis=1)
    steps_log = 0.5 * jnp.log((2.0 * offsets + 3.0) / (2.0 * offsets + 2.0))
    cumulative = jnp.cumsum(steps_log) - steps_log
    picked = jnp.sum(jnp.where(jnp.arange(MODES) == order_value, cumulative, 0.0 * cumulative))
    start_log = 0.5 * math.log(0.5) + picked + order_float * jnp.log(sine_part)
    northern = jnp.exp(start_log[None, :] + log_scale[0]) * matrix[0]
    northern = jnp.where((offsets < MODES - order_float)[:, None], northern, 0.0 * filled)
    parity = jnp.where(jnp.arange(MODES) % 2 == 0, 1.0, -1.0).astype(jnp.float32)
    return jnp.concatenate([northern, northern[:, ::-1] * parity[:, None]], axis=1)

def fourier_tables(orders):
    longitude = jnp.arange(NLON).astype(jnp.int32)
    phase_index = orders[:, None] * longitude[None, :] % NLON
    angles = phase_index.astype(jnp.float32) * (2.0 * math.pi / NLON)
    cosine = jnp.cos(angles)
    sine_part = jnp.sin(angles)
    forward = (jnp.concatenate([cosine, -sine_part], axis=0) * (math.sqrt(2.0 * math.pi) / NLON)).astype(jnp.bfloat16)
    factor = jnp.where(orders == 0, 1.0, 2.0).astype(jnp.float32) / math.sqrt(2.0 * math.pi)
    inverse = jnp.concatenate([cosine * factor[:, None], -sine_part * factor[:, None]], axis=0).astype(jnp.bfloat16)
    return (forward, inverse)

def mixing_blocks(weights):
    real_part = weights[:, 0]
    imag_part = weights[:, 1]
    return jnp.stack([jnp.stack([real_part, imag_part], axis=1), jnp.stack([-imag_part, real_part], axis=1)], axis=1)

def reference(ocean_state, land_mask, order_table, spectral_weight, inner_weight, outer_weight):
    forward, inverse = fourier_tables(order_table)
    flat_state = ocean_state.reshape(NLAT * CHANNELS, NLON)
    coeffs = lax.dot_general(flat_state, forward, (((1,), (1,)), ((), ())), preferred_element_type=jnp.float32)
    coeffs = coeffs.astype(jnp.bfloat16).reshape(NLAT, CHANNELS, 2, MODES)
    per_order = jnp.transpose(coeffs, (3, 0, 1, 2))
    quad_weights = fejer_weights()

    def one_order(inputs):
        order_value, row_coeffs, weight = inputs
        legendre = legendre_rows(order_value)
        weighted = (legendre * quad_weights[None, :]).astype(jnp.bfloat16)
        plain_table = legendre.astype(jnp.bfloat16)
        spectra = jnp.einsum('rcp,kr->pck', row_coeffs.astype(jnp.float32), weighted.astype(jnp.float32)).astype(jnp.bfloat16)
        blocks = mixing_blocks(weight[None])[0]
        mixed_spec = jnp.einsum('pck,pqdc->qdk', spectra.astype(jnp.float32), blocks.astype(jnp.float32)).astype(jnp.bfloat16)
        return jnp.einsum('qdk,kr->rdq', mixed_spec.astype(jnp.float32), plain_table.astype(jnp.float32)).astype(jnp.bfloat16)
    synthesis = lax.map(one_order, (order_table, per_order, spectral_weight))
    synthesis = jnp.transpose(synthesis, (1, 2, 3, 0)).reshape(NLAT * CHANNELS, 2 * MODES)
    spatial = jnp.dot(synthesis, inverse, preferred_element_type=jnp.float32).reshape(NLAT, CHANNELS, NLON)
    hidden = (ocean_state.astype(jnp.float32) + spatial).astype(jnp.bfloat16)
    ocean_mask = land_mask.astype(jnp.float32)

    def one_row(inputs):
        row_hidden, row_mask = inputs
        pre_act = lax.dot_general(row_hidden, inner_weight, (((0,), (0,)), ((), ())), preferred_element_type=jnp.float32)
        activated = jax.nn.gelu(pre_act).astype(jnp.bfloat16)
        update = jnp.dot(activated, outer_weight, preferred_element_type=jnp.float32)
        return (row_mask[:, None] * (jnp.transpose(row_hidden).astype(jnp.float32) + update)).astype(jnp.bfloat16)
    return lax.map(one_row, (hidden, ocean_mask))
```

```python
import functools
import math

import jax
import jax.numpy as jnp
import ml_dtypes
import numpy as np
from jax import lax
from jax.experimental import pallas as pl
from jax.experimental.pallas import tpu as pltpu
from jax.sharding import PartitionSpec as P

NLAT = 384
NLON = 1440
MODES = 384
ZL, YX, CH = 4, 16, 8
SLOTS = 6
ROWS = 6
CHANS = 32
PTS = 96
HALF = 90
LANES = 2 * ROWS * CHANS
BLOCK = 2 * ZL * ROWS
WIDE = YX * BLOCK
GROUPS = WIDE // 128
BF = jnp.bfloat16
F32 = jnp.float32


def bf(a):
    return np.asarray(a, np.float32).astype(ml_dtypes.bfloat16)


@functools.lru_cache(None)
def constants():
    m, j = np.arange(MODES), np.arange(NLON)
    angle = 2 * np.pi * ((m[:, None] * j[None, :]) % NLON) / NLON
    waves = np.stack([np.cos(angle), -np.sin(angle)])
    fwd = bf((waves * (math.sqrt(2 * np.pi) / NLON)).reshape(2 * MODES, NLON))
    factor = np.where(m == 0, 1.0, 2.0) / math.sqrt(2 * np.pi)
    inv = (waves * factor[None, :, None]).reshape(2, MODES, CH, 2, HALF)
    inv = inv.transpose(3, 2, 4, 0, 1)
    inv = np.pad(inv, ((0, 0), (0, 0), (0, PTS - HALF), (0, 0), (0, 0)))
    inv = bf(inv.reshape(2, CH * PTS, 2 * MODES))
    spread = np.zeros((2, CH, PTS, NLON), np.float32)
    for half in range(2):
        for c in range(CH):
            for t in range(HALF):
                spread[half, c, t, 180 * c + HALF * half + t] = 1
    spread = bf(spread.reshape(2, CH * PTS, NLON))
    perm = np.zeros((WIDE, WIDE), np.float32)
    yx, p, zl, r = np.meshgrid(
        np.arange(YX), np.arange(2), np.arange(ZL), np.arange(ROWS), indexing="ij"
    )
    target = ((yx * 2 + p) * ZL + zl) * ROWS + r
    source = ((p * ROWS + r) * ZL + zl) * YX + yx
    perm[target.ravel(), source.ravel()] = 1
    row = (zl * YX + yx) * ROWS + r
    theta_all = (np.arange(NLAT) + 0.5) * np.pi / NLAT
    h = np.arange(1, NLAT // 2 + 1)
    series = np.cos(2 * theta_all[:, None] * h) / (4.0 * h * h - 1)
    quad_all = 2.0 / NLAT * (1 - 2 * series.sum(1))
    theta = theta_all[row.ravel()]
    geo = np.zeros((2, 8, 128), np.float32)
    geo[0, :GROUPS] = np.cos(theta).reshape(GROUPS, 128)
    geo[1, :GROUPS] = np.log(np.sin(theta)).reshape(GROUPS, 128)
    quad = np.stack([quad_all[row.ravel()] * (p.ravel() == k) for k in range(2)])
    q = np.arange(1, MODES)
    cum = np.concatenate([[0.0], np.cumsum(0.5 * np.log((2.0 * q + 1) / (2.0 * q)))])
    return (
        fwd,
        inv,
        spread,
        bf(perm),
        bf(perm.T),
        geo,
        quad.astype(np.float32),
        cum.astype(np.float32)[None],
    )


def dot(a, b, ca=1, cb=0):
    return lax.dot_general(a, b, (((ca,), (cb,)), ((), ())), preferred_element_type=F32)


def spectral(
    ord_s, ord_c, ord_l, x, geo, quad, cum, fwd_h, inv_h, spread_h, perm_h, permt_h, w_h,
    out,
    fwd, inv, spread, perm, permt, wk, s1, r1, tmp, s2, r2, mix, s3, r3, tmp2, s4, r4, ym, xt, s5, r5,
    acoef, ucoef, table, weighted, plain_t,
    lsem, wsend, wrecv, s1s, s1r, s2s, s2r, s3s, s3r, s4s, s4r, s5s, s5r,
):
    lat, ch = lax.axis_index("lat"), lax.axis_index("chan")
    zl, yx = lat // YX, lax.rem(lat, YX)
    active = lax.rem(ch, 4) != 3
    slot = ch - ch // 4

    def chan_of(s):
        return s + s // 3

    def z_peer(i):
        return (i // CH) * YX + yx, lax.rem(i, CH)

    def z_holder(i):
        return (i // SLOTS) * YX + yx, chan_of(lax.rem(i, SLOTS))

    def xy_peer(i):
        return zl * YX + i, ch

    def chan_peer(i):
        return lat, i

    def chan_holder(i):
        return lat, chan_of(i)

    def remote(src, dst, ssem, rsem, to):
        return pltpu.make_async_remote_copy(
            src_ref=src, dst_ref=dst, send_sem=ssem, recv_sem=rsem,
            device_id=to, device_id_type=pl.DeviceIdType.MESH,
        )

    def send(n, start, peer, src, dst, ssem, rsem):
        def body(i, carry):
            t = lax.rem(i + start, n)
            to = peer(t)
            mine = (to[0] == lat) & (to[1] == ch)

            @pl.when(jnp.logical_not(mine))
            def _():
                remote(src(t), dst, ssem.at[t], rsem, to).start()

            @pl.when(mine)
            def _():
                pltpu.make_async_copy(src(t), dst, rsem).start()

            return carry

        lax.fori_loop(0, n, body, 0)

    def sent(n, peer, src, dst, ssem, rsem):
        def body(t, carry):
            to = peer(t)

            @pl.when((to[0] != lat) | (to[1] != ch))
            def _():
                remote(src(t), dst, ssem.at[t], rsem, to).wait_send()

            return carry

        lax.fori_loop(0, n, body, 0)

    def received(n, dst, rsem):
        def body(t, carry):
            pltpu.make_async_copy(dst(t), dst(t), rsem.at[t]).wait()
            return carry

        lax.fori_loop(0, n, body, 0)

    loads = [
        pltpu.make_async_copy(a, b, lsem.at[k])
        for k, (a, b) in enumerate(
            ((fwd_h, fwd), (perm_h, perm), (spread_h, spread), (permt_h, permt), (inv_h, inv))
        )
    ]
    for load in loads:
        load.start()

    barrier = pltpu.get_barrier_semaphore()

    def greet(n, peer):
        def body(i, carry):
            to = peer(i)

            @pl.when((to[0] != lat) | (to[1] != ch))
            def _():
                pl.semaphore_signal(
                    barrier, inc=1, device_id=to, device_id_type=pl.DeviceIdType.MESH
                )

            return carry

        lax.fori_loop(0, n, body, 0)

    greet(ZL * CH, z_peer)
    greet(YX, xy_peer)

    loads[0].wait()
    parts = [dot(fwd[k * MODES : (k + 1) * MODES, :], x[...], 1, 1) for k in range(2)]
    coeffs = jnp.concatenate(parts, axis=1).astype(BF)
    natural = lax.broadcasted_iota(jnp.int32, (MODES, MODES), 1)
    select = jnp.where(natural == ord_c[...], 1.0, 0.0).astype(BF)
    s1[...] = dot(select, coeffs).astype(BF).reshape(ZL * SLOTS, YX, LANES)

    pl.semaphore_wait(barrier, ZL * CH - 1 + YX - 1)
    me_z = zl * CH + ch
    me_slot = zl * SLOTS + slot
    send(ZL * SLOTS, zl * SLOTS + lax.rem(ch, SLOTS), z_holder,
         lambda t: s1.at[t], r1.at[me_z], s1s, s1r.at[me_z])
    send(SLOTS, lax.rem(ch, SLOTS), chan_holder,
         lambda t: w_h.at[t], wk.at[ch], wsend, wrecv.at[ch])

    loads[2].wait()
    for half in range(2):
        xt[half] = dot(spread[half], x[...], 1, 1).astype(BF)

    @pl.when(active)
    def _():
        order = ord_s[lat * SLOTS + slot].astype(F32)
        i = lax.broadcasted_iota(jnp.int32, (MODES, 128), 0).astype(F32)
        later = i >= 1.0
        degree = order + i
        low = i - 1.0
        prev = degree - 1.0
        a = jnp.sqrt(
            (4.0 * degree * degree - 1.0) / jnp.where(later, i * (2.0 * order + i), 1.0)
        )
        b = jnp.sqrt(
            jnp.maximum(low * (2.0 * order + low), 0.0)
            / jnp.maximum(4.0 * prev * prev - 1.0, 1.0)
        )
        acoef[...] = jnp.where(later, a, 0.0)
        ucoef[...] = jnp.where(later, a * b, 1.0)
        m_of = lax.broadcasted_iota(jnp.int32, (1, MODES), 1).astype(F32)
        picked = jnp.sum(jnp.where(m_of == order, cum[...], 0.0), axis=1, keepdims=True)
        cosine = geo[0]
        log_first = order * geo[1] + (picked + 0.5 * math.log(0.5))

        def steps(t, carry):
            one, two, log_now = carry
            factor = jnp.exp(log_now)
            for s in range(8):
                k = t * 8 + s
                now = acoef[pl.ds(k, 1), :] * cosine * one - ucoef[pl.ds(k, 1), :] * two
                table[pl.ds(pl.multiple_of(k * 8, 8), 8), :] = now * factor
                one, two = now, one
            big = jnp.maximum(jnp.abs(one), jnp.abs(two)) > 2.0**40
            shrink = jnp.where(big, 2.0**-40, 1.0)
            log_now = log_now + jnp.where(big, 40.0 * math.log(2.0), 0.0)
            return one * shrink, two * shrink, log_now

        lax.fori_loop(
            0, MODES // 8, steps,
            (jnp.zeros((8, 128), F32), jnp.full((8, 128), -1.0, F32), log_first),
        )
        valid = i < MODES - order
        for g in range(GROUPS):
            lanes = slice(g * 128, (g + 1) * 128)
            part = jnp.where(valid, table[pl.ds(g, MODES, stride=8), :], 0.0)
            for p in range(2):
                weighted[p, :, lanes] = (part * quad[p : p + 1, lanes]).astype(BF)
            turned = part.T
            row = lax.broadcasted_iota(jnp.int32, (128, MODES), 0) + g * 128
            which = lax.rem(row // (BLOCK // 2), 2)
            for p in range(2):
                plain_t[lanes, p * MODES : (p + 1) * MODES] = jnp.where(
                    which == p, turned, 0.0
                ).astype(BF)

        received(ZL * CH, lambda t: r1.at[t], s1r)
        blocks = [
            jnp.concatenate([r1[z * CH + c] for z in range(ZL)], axis=0) for c in range(CH)
        ]
        for k in range(2 * ROWS):
            tmp[k * ZL * YX : (k + 1) * ZL * YX, :] = jnp.concatenate(
                [blocks[c][:, k * CHANS : (k + 1) * CHANS] for c in range(CH)], axis=1
            )
        loads[1].wait()
        s2[...] = dot(perm[...], tmp[...]).astype(BF).reshape(YX, BLOCK, CH * CHANS)
        send(YX, yx, xy_peer, lambda t: s2.at[t], r2.at[yx], s2s, s2r.at[yx])
        received(CH, lambda t: wk.at[t], wrecv)
        received(YX, lambda t: r2.at[t], s2r)
        field = r2[...].reshape(WIDE, CH * CHANS)
        real, imag = (dot(weighted[p], field).astype(BF) for p in range(2))
        w_real = wk[:, 0].reshape(CH * CHANS, CH * CHANS)
        w_imag = wk[:, 1].reshape(CH * CHANS, CH * CHANS)
        mix[0:MODES, :] = (dot(real, w_real, 1, 1) - dot(imag, w_imag, 1, 1)).astype(BF)
        mix[MODES:, :] = (dot(real, w_imag, 1, 1) + dot(imag, w_real, 1, 1)).astype(BF)
        s3[...] = dot(plain_t[...], mix[...]).astype(BF).reshape(YX, BLOCK, CH * CHANS)
        send(YX, yx, xy_peer, lambda t: s3.at[t], r3.at[yx], s3s, s3r.at[yx])
        loads[3].wait()
        received(YX, lambda t: r3.at[t], s3r)
        tmp2[...] = dot(permt[...], r3[...].reshape(WIDE, CH * CHANS)).astype(BF)
        for c in range(CH):
            piece = jnp.concatenate(
                [
                    tmp2[k * ZL * YX : (k + 1) * ZL * YX, c * CHANS : (c + 1) * CHANS]
                    for k in range(2 * ROWS)
                ],
                axis=1,
            )
            for z in range(ZL):
                s4[z * CH + c] = piece[z * YX : (z + 1) * YX, :]
        send(ZL * CH, me_z, z_peer, lambda t: s4.at[t], r4.at[me_slot], s4s, s4r.at[me_slot])

    @pl.when(jnp.logical_not(active))
    def _():
        loads[1].wait()
        loads[3].wait()

    slot_of = lax.broadcasted_iota(jnp.int32, (MODES, MODES), 0)
    unselect = jnp.where(slot_of == ord_l[...], 1.0, 0.0).astype(BF)
    loads[4].wait()
    received(ZL * SLOTS, lambda t: r4.at[t], s4r)
    held = dot(unselect, r4[...].reshape(MODES, LANES)).astype(BF)
    ym[0:MODES, :] = held[:, : LANES // 2]
    ym[MODES:, :] = held[:, LANES // 2 :]
    halves = [
        (dot(inv[half], ym[...]) + xt[half].astype(F32)).astype(BF) for half in range(2)
    ]
    s5[...] = jnp.concatenate(halves, axis=1).reshape(CH, PTS, LANES)
    send(CH, ch, chan_peer, lambda t: s5.at[t], r5.at[ch], s5s, s5r.at[ch])
    received(CH, lambda t: r5.at[t], s5r)
    out[...] = r5[...]

    sent(ZL * SLOTS, z_holder, lambda t: s1.at[t], r1.at[me_z], s1s, s1r.at[me_z])
    sent(SLOTS, chan_holder, lambda t: w_h.at[t], wk.at[ch], wsend, wrecv.at[ch])

    @pl.when(active)
    def _():
        sent(YX, xy_peer, lambda t: s2.at[t], r2.at[yx], s2s, s2r.at[yx])
        sent(YX, xy_peer, lambda t: s3.at[t], r3.at[yx], s3s, s3r.at[yx])
        sent(ZL * CH, z_peer, lambda t: s4.at[t], r4.at[me_slot], s4s, s4r.at[me_slot])

    sent(CH, chan_peer, lambda t: s5.at[t], r5.at[ch], s5s, s5r.at[ch])


def spectral_call(order_table, flat_state, spectral_weight):
    fwd, inv, spread, perm, permt, geo, quad, cum = constants()
    slots = order_table.reshape(ZL, YX, SLOTS).transpose(0, 2, 1).reshape(-1)
    vmem = pl.BlockSpec(memory_space=pltpu.VMEM)
    anywhere = pl.BlockSpec(memory_space=pl.ANY)
    sem = pltpu.SemaphoreType.DMA
    full = CH * CHANS
    return pl.pallas_call(
        spectral,
        out_shape=jax.ShapeDtypeStruct((CH, PTS, LANES), BF),
        in_specs=[pl.BlockSpec(memory_space=pltpu.SMEM)] + [vmem] * 6 + [anywhere] * 6,
        out_specs=vmem,
        scratch_shapes=[
            pltpu.VMEM(fwd.shape, BF),
            pltpu.VMEM(inv.shape, BF),
            pltpu.VMEM(spread.shape, BF),
            pltpu.VMEM(perm.shape, BF),
            pltpu.VMEM(perm.shape, BF),
            pltpu.VMEM((CH, 2, CHANS, full), BF),
            pltpu.VMEM((ZL * SLOTS, YX, LANES), BF),
            pltpu.VMEM((ZL * CH, YX, LANES), BF),
            pltpu.VMEM((WIDE, full), BF),
            pltpu.VMEM((YX, BLOCK, full), BF),
            pltpu.VMEM((YX, BLOCK, full), BF),
            pltpu.VMEM((2 * MODES, full), BF),
            pltpu.VMEM((YX, BLOCK, full), BF),
            pltpu.VMEM((YX, BLOCK, full), BF),
            pltpu.VMEM((WIDE, full), BF),
            pltpu.VMEM((ZL * CH, YX, LANES), BF),
            pltpu.VMEM((ZL * SLOTS, YX, LANES), BF),
            pltpu.VMEM((2 * MODES, LANES // 2), BF),
            pltpu.VMEM((2, CH * PTS, LANES // 2), BF),
            pltpu.VMEM((CH, PTS, LANES), BF),
            pltpu.VMEM((CH, PTS, LANES), BF),
            pltpu.VMEM((MODES, 128), F32),
            pltpu.VMEM((MODES, 128), F32),
            pltpu.VMEM((MODES * 8, 128), F32),
            pltpu.VMEM((2, MODES, WIDE), BF),
            pltpu.VMEM((WIDE, 2 * MODES), BF),
            sem((5,)),
            sem((SLOTS,)),
            sem((CH,)),
            sem((ZL * SLOTS,)),
            sem((ZL * CH,)),
            sem((YX,)),
            sem((YX,)),
            sem((YX,)),
            sem((YX,)),
            sem((ZL * CH,)),
            sem((ZL * SLOTS,)),
            sem((CH,)),
            sem((CH,)),
        ],
        compiler_params=pltpu.CompilerParams(
            collective_id=0, has_side_effects=True, vmem_limit_bytes=48 * 2**20
        ),
        cost_estimate=pl.CostEstimate(
            flops=2 * 10**9, bytes_accessed=12 * 10**6, transcendentals=10**5
        ),
    )(
        order_table, slots[:, None], slots[None, :], flat_state, geo, quad, cum,
        fwd, inv, spread, perm, permt, spectral_weight,
    )


def mlp(field, weights, out):
    inner = weights[:, :64, :].reshape(512, 256)
    outer = weights[:, 64:, :].reshape(512, 256)
    for k in range(2 * ROWS):
        hidden = jnp.concatenate(
            [field[c, :, k * CHANS : (k + 1) * CHANS] for c in range(CH)], axis=1
        )
        activated = jax.nn.gelu(dot(hidden, inner, 1, 1)).astype(BF)
        out[k] = (hidden.astype(F32) + dot(activated, outer)).astype(BF)


def local(ocean_state, land_mask, order_table, spectral_weight, inner_weight, outer_weight):
    own = jnp.concatenate([inner_weight.T, outer_weight], axis=0)
    weights = lax.all_gather(own, "chan", axis=0)
    flat_state = ocean_state.reshape(ROWS * CHANS, NLON)
    field = spectral_call(order_table, flat_state, spectral_weight)
    points = pl.pallas_call(
        mlp,
        out_shape=jax.ShapeDtypeStruct((2 * ROWS, PTS, 256), BF),
        compiler_params=pltpu.CompilerParams(vmem_limit_bytes=32 * 2**20),
    )(field, weights)
    points = points.reshape(2, ROWS, PTS, 256)[:, :, :HALF].transpose(1, 0, 2, 3)
    points = points.reshape(ROWS, 2 * HALF, 256)
    return (land_mask.astype(F32)[:, :, None] * points.astype(F32)).astype(BF)


def solution(mesh):
    placed = (
        P("lat", "chan", None),
        P("lat", "chan"),
        P(),
        P("lat", None, "chan", None),
        P(None, "chan"),
        P("chan", None),
    )
    return jax.shard_map(
        local, mesh=mesh, in_specs=placed, out_specs=P("lat", "chan", None), check_vma=False
    )
```

```python
import functools
import math

import jax
import jax.numpy as jnp
import ml_dtypes
import numpy as np
from jax import lax
from jax.experimental import pallas as pl
from jax.experimental.pallas import tpu as pltpu
from jax.sharding import PartitionSpec as P

NLAT = 384
NLON = 1440
MODES = 384
ZL, YX, CH = 4, 16, 8
SLOTS = 6
ROWS, CHANS, FFN = 6, 32, 512
FULL = CH * CHANS
GROUPS, PAIR = 3, 2
PTS = 96
HALF = 90
LANES = 2 * PAIR * CHANS
BLOCK = 2 * ZL * PAIR
WIDE = YX * BLOCK
TILES = YX
BF = jnp.bfloat16
F32 = jnp.float32


def bf(a):
    return np.asarray(a, np.float32).astype(ml_dtypes.bfloat16)


@functools.lru_cache(None)
def constants():
    m, j = np.arange(MODES), np.arange(NLON)
    angle = 2 * np.pi * ((m[:, None] * j[None, :]) % NLON) / NLON
    waves = np.stack([np.cos(angle), -np.sin(angle)])
    fwd = bf((waves * (math.sqrt(2 * np.pi) / NLON)).reshape(2 * MODES, NLON))
    factor = np.where(m == 0, 1.0, 2.0) / math.sqrt(2 * np.pi)
    inv = (waves * factor[None, :, None]).reshape(2, MODES, CH, 2, HALF)
    inv = inv.transpose(3, 2, 4, 0, 1)
    inv = np.pad(inv, ((0, 0), (0, 0), (0, PTS - HALF), (0, 0), (0, 0)))
    inv = bf(inv.reshape(2, CH * PTS, 2 * MODES))
    spread = np.zeros((2, CH, PTS, NLON), np.float32)
    for half in range(2):
        for c in range(CH):
            for t in range(HALF):
                spread[half, c, t, 180 * c + HALF * half + t] = 1
    spread = bf(spread.reshape(2, CH * PTS, NLON))
    perm = np.zeros((WIDE, WIDE), np.float32)
    yx, p, zl, r = np.meshgrid(
        np.arange(YX), np.arange(2), np.arange(ZL), np.arange(PAIR), indexing="ij"
    )
    target = ((yx * 2 + p) * ZL + zl) * PAIR + r
    source = ((p * PAIR + r) * ZL + zl) * YX + yx
    perm[target.ravel(), source.ravel()] = 1
    slots = np.arange(MODES).reshape(ZL, YX, SLOTS).transpose(0, 2, 1).ravel()
    shuffle = np.zeros((MODES, MODES), np.float32)
    shuffle[np.arange(MODES), slots] = 1
    first = (zl * YX + yx) * ROWS + r
    row = np.concatenate([(first + PAIR * g).ravel() for g in range(GROUPS)])
    part = np.tile(p.ravel(), GROUPS)
    theta_all = (np.arange(NLAT) + 0.5) * np.pi / NLAT
    h = np.arange(1, NLAT // 2 + 1)
    series = np.cos(2 * theta_all[:, None] * h) / (4.0 * h * h - 1)
    quad_all = 2.0 / NLAT * (1 - 2 * series.sum(1))
    theta = theta_all[row]
    q = np.arange(1, MODES)
    aux = np.zeros((32, GROUPS * WIDE), np.float32)
    aux[0:6, :128] = np.cos(theta).reshape(6, 128)
    aux[8:14, :128] = np.log(np.sin(theta)).reshape(6, 128)
    aux[16] = quad_all[row] * (part == 0)
    aux[17] = quad_all[row] * (part == 1)
    aux[24, 1:MODES] = np.cumsum(0.5 * np.log((2.0 * q + 1) / (2.0 * q)))
    return fwd, inv, spread, bf(perm), bf(perm.T), bf(shuffle), aux


def dot(a, b, ca=1, cb=0):
    return lax.dot_general(a, b, (((ca,), (cb,)), ((), ())), preferred_element_type=F32)


def layer(
    ord_v, mask, x_h, aux_h, fwd_h, shuffle_h, perm_h, permt_h, spread_h, inv_h, w_h, inner_h, outer_h,
    out,
    x, aux, fwd, shuffle, perm, permt, spread, inv, wk, wa, wb, inner, outer, turned_mask,
    s1, r1, tmp, s2, r2, mix, s3, r3, s4, r4, ym, xt, s5, r5,
    acoef, ucoef, table, weighted, plain_t,
    lsem, wsend, wrecv, asend, arecv, bsend, brecv,
    s1s, s1r, s2s, s2r, s3s, s3r, s4s, s4r, s5s, s5r,
):
    lat, ch = lax.axis_index("lat"), lax.axis_index("chan")
    zl, yx = lat // YX, lax.rem(lat, YX)
    active = lax.rem(ch, 4) != 3
    slot = ch - ch // 4
    me_z = zl * CH + ch
    me_slot = zl * SLOTS + slot

    def chan_of(s):
        return s + s // 3

    def z_peer(i):
        return (i // CH) * YX + yx, lax.rem(i, CH)

    def z_holder(i):
        return (i // SLOTS) * YX + yx, chan_of(lax.rem(i, SLOTS))

    def xy_peer(i):
        return zl * YX + i, ch

    def chan_peer(i):
        return lat, i

    def chan_holder(i):
        return lat, chan_of(i)

    def send(n, start, peer, src, dst, ssem, rsem):
        def body(i, carry):
            t = lax.rem(i + start, n)
            to = peer(t)
            mine = (to[0] == lat) & (to[1] == ch)

            @pl.when(jnp.logical_not(mine))
            def _():
                pltpu.make_async_remote_copy(
                    src_ref=src(t), dst_ref=dst, send_sem=ssem, recv_sem=rsem,
                    device_id=to, device_id_type=pl.DeviceIdType.MESH,
                ).start()

            @pl.when(mine)
            def _():
                pltpu.make_async_copy(src(t), dst, rsem).start()

            return carry

        lax.fori_loop(0, n, body, 0)

    def wait(ref, sem):
        pltpu.make_async_copy(ref, ref, sem).wait()

    loads = [
        pltpu.make_async_copy(a, b, lsem.at[k])
        for k, (a, b) in enumerate(
            (
                (x_h, x), (fwd_h, fwd), (shuffle_h, shuffle), (aux_h, aux), (spread_h, spread),
                (perm_h, perm), (permt_h, permt), (inv_h, inv),
            )
        )
    ]
    for load in loads[:4]:
        load.start()

    barrier = pltpu.get_barrier_semaphore()

    def greet(n, peer):
        def body(i, carry):
            to = peer(i)

            @pl.when((to[0] != lat) | (to[1] != ch))
            def _():
                pl.semaphore_signal(
                    barrier, inc=1, device_id=to, device_id_type=pl.DeviceIdType.MESH
                )

            return carry

        lax.fori_loop(0, n, body, 0)

    greet(ZL * CH, z_peer)
    greet(YX, xy_peer)
    for load in loads[4:]:
        load.start()

    natural = lax.broadcasted_iota(jnp.int32, (MODES, MODES), 0)
    orders = ord_v[...].reshape(1, MODES)
    one_hot = jnp.where(natural == orders, 1.0, 0.0).astype(BF)
    loads[2].wait()
    select = dot(shuffle[...], one_hot, 1, 1).astype(BF)
    loads[0].wait()
    loads[1].wait()
    parts = [dot(fwd[k * MODES : (k + 1) * MODES, :], x[...], 1, 1) for k in range(2)]
    wide = PAIR * CHANS
    coeffs = jnp.concatenate(
        [parts[p][:, g * wide : (g + 1) * wide] for g in range(GROUPS) for p in range(2)], axis=1
    ).astype(BF)
    chosen = dot(select, coeffs).astype(BF)
    for g in range(GROUPS):
        lanes = slice(g * LANES, (g + 1) * LANES)
        s1[g] = chosen[:, lanes].reshape(ZL * SLOTS, YX, LANES)

    pl.semaphore_wait(barrier, ZL * CH - 1 + YX - 1)

    def send_mixing(p):
        send(SLOTS, lax.rem(ch, SLOTS), chan_holder,
             lambda t: w_h.at[t, p], wk.at[p, ch], wsend.at[p], wrecv.at[p])

    for g in range(GROUPS):
        send(ZL * SLOTS, zl * SLOTS + lax.rem(ch, SLOTS), z_holder,
             lambda t: s1.at[g, t], r1.at[g, me_z], s1s.at[g], s1r.at[g])
    tile_row = pl.multiple_of(lax.rem(yx // 2, 4) * 16, 16)
    tile_lane = pl.multiple_of(lax.rem(yx, 2) * 128, 128)

    @pl.when(yx < TILES // 2)
    def _():
        send(CH, ch, chan_peer, lambda t: inner_h.at[pl.ds(tile_row, 16), pl.ds(tile_lane, 128)],
             wa.at[ch], asend, arecv)

    @pl.when(yx >= TILES // 2)
    def _():
        send(CH, ch, chan_peer, lambda t: outer_h.at[pl.ds(tile_row, 16), pl.ds(tile_lane, 128)],
             wa.at[ch], asend, arecv)

    send_mixing(0)

    loads[4].wait()
    moved = [dot(spread[half], x[...], 1, 1) for half in range(2)]
    for g in range(GROUPS):
        xt[g] = jnp.concatenate(
            [moved[half][:, g * wide : (g + 1) * wide] for half in range(2)], axis=1
        ).astype(BF)
    loads[3].wait()
    padded = jnp.concatenate([mask[...].astype(F32), jnp.zeros((ROWS, 76), F32)], axis=1)
    padded = jnp.concatenate([padded, jnp.zeros((8 - ROWS, 256), F32)], axis=0)
    turned_mask[...] = padded.T

    @pl.when(active)
    def _():
        held = lax.broadcasted_iota(jnp.int32, (1, MODES), 1) == lat * SLOTS + slot
        order = jnp.sum(jnp.where(held, orders.astype(F32), 0.0), axis=1, keepdims=True)
        i = lax.broadcasted_iota(jnp.int32, (MODES, 128), 0).astype(F32)
        later = i >= 1.0
        degree = order + i
        low = i - 1.0
        prev = degree - 1.0
        a = jnp.sqrt(
            (4.0 * degree * degree - 1.0) / jnp.where(later, i * (2.0 * order + i), 1.0)
        )
        b = jnp.sqrt(
            jnp.maximum(low * (2.0 * order + low), 0.0)
            / jnp.maximum(4.0 * prev * prev - 1.0, 1.0)
        )
        acoef[...] = jnp.where(later, a, 0.0)
        ucoef[...] = jnp.where(later, a * b, 1.0)
        m_of = lax.broadcasted_iota(jnp.int32, (1, MODES), 1).astype(F32)
        picked = jnp.sum(
            jnp.where(m_of == order, aux[24:25, :MODES], 0.0), axis=1, keepdims=True
        )
        cosine = aux[0:8, :128]
        log_first = order * aux[8:16, :128] + (picked + 0.5 * math.log(0.5))

        def steps(t, carry):
            one, two, log_now = carry
            factor = jnp.exp(log_now)
            for s in range(8):
                k = t * 8 + s
                now = acoef[pl.ds(k, 1), :] * cosine * one - ucoef[pl.ds(k, 1), :] * two
                table[pl.ds(pl.multiple_of(k * 8, 8), 8), :] = now * factor
                one, two = now, one
            big = jnp.maximum(jnp.abs(one), jnp.abs(two)) > 2.0**40
            shrink = jnp.where(big, 2.0**-40, 1.0)
            log_now = log_now + jnp.where(big, 40.0 * math.log(2.0), 0.0)
            return one * shrink, two * shrink, log_now

        lax.fori_loop(
            0, MODES // 8, steps,
            (jnp.zeros((8, 128), F32), jnp.full((8, 128), -1.0, F32), log_first),
        )
        valid = i < MODES - order
        for k in range(GROUPS * WIDE // 128):
            lanes = slice(k * 128, (k + 1) * 128)
            part = jnp.where(valid, table[pl.ds(k, MODES, stride=8), :], 0.0)
            for p in range(2):
                weighted[p, :, lanes] = (part * aux[16 + p : 17 + p, lanes]).astype(BF)
            turned = part.T
            row = lax.broadcasted_iota(jnp.int32, (128, MODES), 0)
            which = lax.rem(row // (BLOCK // 2), 2)
            for p in range(2):
                plain_t[lanes, p * MODES : (p + 1) * MODES] = jnp.where(
                    which == p, turned, 0.0
                ).astype(BF)

    wait(wa, arecv)
    send(YX, yx, xy_peer, lambda t: wa, wb.at[yx], bsend, brecv)
    loads[5].wait()
    loads[6].wait()

    @pl.when(active)
    def _():
        for g in range(GROUPS):
            wait(r1.at[g], s1r.at[g])
            blocks = [
                jnp.concatenate([r1[g, z * CH + c] for z in range(ZL)], axis=0)
                for c in range(CH)
            ]
            for k in range(2 * PAIR):
                tmp[k * ZL * YX : (k + 1) * ZL * YX, :] = jnp.concatenate(
                    [blocks[c][:, k * CHANS : (k + 1) * CHANS] for c in range(CH)], axis=1
                )
            s2[g] = dot(perm[...], tmp[...]).astype(BF).reshape(YX, BLOCK, FULL)
            send(YX, yx, xy_peer, lambda t: s2.at[g, t], r2.at[g, yx], s2s.at[g], s2r.at[g])

    send_mixing(1)

    @pl.when(active)
    def _():
        spectra = [0.0, 0.0]
        for g in range(GROUPS):
            wait(r2.at[g], s2r.at[g])
            field = r2[g].reshape(WIDE, FULL)
            for p in range(2):
                spectra[p] += dot(weighted[p, :, g * WIDE : (g + 1) * WIDE], field)
        real, imag = (v.astype(BF) for v in spectra)
        for p in range(2):
            wait(wk.at[p], wrecv.at[p])
        w_real = wk[0].reshape(FULL, FULL)
        w_imag = wk[1].reshape(FULL, FULL)
        mix[0:MODES, :] = (dot(real, w_real, 1, 1) - dot(imag, w_imag, 1, 1)).astype(BF)
        mix[MODES:, :] = (dot(real, w_imag, 1, 1) + dot(imag, w_real, 1, 1)).astype(BF)
        for g in range(GROUPS):
            rows = slice(g * WIDE, (g + 1) * WIDE)
            s3[g] = dot(plain_t[rows, :], mix[...]).astype(BF).reshape(YX, BLOCK, FULL)
            send(YX, yx, xy_peer, lambda t: s3.at[g, t], r3.at[g, yx], s3s.at[g], s3r.at[g])
        for g in range(GROUPS):
            wait(r3.at[g], s3r.at[g])
            back = dot(permt[...], r3[g].reshape(WIDE, FULL)).astype(BF)
            for c in range(CH):
                piece = jnp.concatenate(
                    [
                        back[k * ZL * YX : (k + 1) * ZL * YX, c * CHANS : (c + 1) * CHANS]
                        for k in range(2 * PAIR)
                    ],
                    axis=1,
                )
                for z in range(ZL):
                    s4[g, z * CH + c] = piece[z * YX : (z + 1) * YX, :]
            send(ZL * CH, me_z, z_peer,
                 lambda t: s4.at[g, t], r4.at[g, me_slot], s4s.at[g], s4r.at[g])

    unselect = dot(one_hot, shuffle[...], 1, 1).astype(BF)
    wait(wb, brecv)
    for t in range(TILES):
        whole = inner if t < TILES // 2 else outer
        a, b = (t // 2) % 4 * 16, t % 2 * 128
        whole[:, a : a + 16, b : b + 128] = wb[t]
    loads[7].wait()
    for g in range(GROUPS):
        wait(r4.at[g], s4r.at[g])
        held = dot(unselect, r4[g].reshape(MODES, LANES)).astype(BF)
        ym[0:MODES, :] = held[:, :wide]
        ym[MODES:, :] = held[:, wide:]
        both = jnp.concatenate([dot(inv[half], ym[...]) for half in range(2)], axis=1)
        s5[g] = (both + xt[g].astype(F32)).astype(BF).reshape(CH, PTS, LANES)
        send(CH, ch, chan_peer, lambda t: s5.at[g, t], r5.at[g, ch], s5s.at[g], s5r.at[g])

    inner_all = inner[...].reshape(FFN, FULL)
    outer_all = outer[...].reshape(FFN, FULL)
    for g in range(GROUPS):
        wait(r5.at[g], s5r.at[g])
        hidden = jnp.concatenate(
            [
                jnp.concatenate(
                    [r5[g, c, :, k * CHANS : (k + 1) * CHANS] for c in range(CH)], axis=1
                )
                for k in range(2 * PAIR)
            ],
            axis=0,
        )
        activated = jax.nn.gelu(dot(hidden, inner_all, 1, 1)).astype(BF)
        total = hidden.astype(F32) + dot(activated, outer_all)
        for r in range(PAIR):
            row = PAIR * g + r
            points = jnp.concatenate(
                [
                    total[(half * PAIR + r) * PTS : (half * PAIR + r) * PTS + HALF, :]
                    for half in range(2)
                ],
                axis=0,
            )
            out[row] = (points * turned_mask[0 : 2 * HALF, row : row + 1]).astype(BF)

    for p in range(2):
        others = w_h.at[pl.ds(0, SLOTS - 1), p]

        @pl.when(active)
        def _():
            wait(others, wsend.at[p])

        @pl.when(jnp.logical_not(active))
        def _():
            wait(w_h.at[:, p], wsend.at[p])

    wait(wa.at[pl.ds(0, CH - 1)], asend)
    wait(wb.at[pl.ds(0, YX - 1)], bsend)
    for g in range(GROUPS):
        wait(s5.at[g, pl.ds(0, CH - 1)], s5s.at[g])

        @pl.when(active)
        def _():
            wait(s1.at[g, pl.ds(0, ZL * SLOTS - 1)], s1s.at[g])
            wait(s2.at[g, pl.ds(0, YX - 1)], s2s.at[g])
            wait(s3.at[g, pl.ds(0, YX - 1)], s3s.at[g])
            wait(s4.at[g, pl.ds(0, ZL * CH - 1)], s4s.at[g])

        @pl.when(jnp.logical_not(active))
        def _():
            wait(s1.at[g], s1s.at[g])


def local(ocean_state, land_mask, order_table, spectral_weight, inner_weight, outer_weight):
    fwd, inv, spread, perm, permt, shuffle, aux = constants()
    flat_state = ocean_state.reshape(ROWS * CHANS, NLON)
    vmem = pl.BlockSpec(memory_space=pltpu.VMEM)
    anywhere = pl.BlockSpec(memory_space=pl.ANY)
    sem = pltpu.SemaphoreType.DMA
    z_out, z_in = (ZL * SLOTS, YX, LANES), (ZL * CH, YX, LANES)

    def held(*shape):
        return pltpu.VMEM(shape, BF)

    return pl.pallas_call(
        layer,
        out_shape=jax.ShapeDtypeStruct((ROWS, 2 * HALF, FULL), BF),
        in_specs=[vmem] * 2 + [anywhere] * 11,
        out_specs=vmem,
        scratch_shapes=[
            held(*flat_state.shape),
            pltpu.VMEM(aux.shape, F32),
            held(*fwd.shape),
            held(*shuffle.shape),
            held(*perm.shape),
            held(*perm.shape),
            held(*spread.shape),
            held(*inv.shape),
            held(2, CH, CHANS, FULL),
            held(CH, 16, 128),
            held(YX, CH, 16, 128),
            held(CH, FFN // CH, FULL),
            held(CH, FFN // CH, FULL),
            pltpu.VMEM((256, 8), F32),
            held(GROUPS, *z_out),
            held(GROUPS, *z_in),
            held(WIDE, FULL),
            held(GROUPS, YX, BLOCK, FULL),
            held(GROUPS, YX, BLOCK, FULL),
            held(2 * MODES, FULL),
            held(GROUPS, YX, BLOCK, FULL),
            held(GROUPS, YX, BLOCK, FULL),
            held(GROUPS, *z_in),
            held(GROUPS, *z_out),
            held(2 * MODES, LANES // 2),
            held(GROUPS, CH * PTS, LANES),
            held(GROUPS, CH, PTS, LANES),
            held(GROUPS, CH, PTS, LANES),
            pltpu.VMEM((MODES, 128), F32),
            pltpu.VMEM((MODES, 128), F32),
            pltpu.VMEM((MODES * 8, 128), F32),
            held(2, MODES, GROUPS * WIDE),
            held(GROUPS * WIDE, 2 * MODES),
            sem((8,)),
            sem((2,)),
            sem((2,)),
            sem,
            sem,
            sem,
            sem,
        ]
        + [sem((GROUPS,))] * 10,
        compiler_params=pltpu.CompilerParams(
            collective_id=0, has_side_effects=True, vmem_limit_bytes=60 * 2**20
        ),
        cost_estimate=pl.CostEstimate(
            flops=2 * 10**9, bytes_accessed=12 * 10**6, transcendentals=10**5
        ),
    )(
        order_table, land_mask, flat_state, aux, fwd, shuffle, perm, permt, spread, inv,
        spectral_weight, inner_weight.T, outer_weight,
    )


def solution(mesh):
    placed = (
        P("lat", "chan", None),
        P("lat", "chan"),
        P(),
        P("lat", None, "chan", None),
        P(None, "chan"),
        P("chan", None),
    )
    return jax.shard_map(
        local, mesh=mesh, in_specs=placed, out_specs=P("lat", "chan", None), check_vma=False
    )
```

```python
import functools
import math

import jax
import jax.numpy as jnp
import ml_dtypes
import numpy as np
from jax import lax
from jax.experimental import pallas as pl
from jax.experimental.pallas import tpu as pltpu
from jax.sharding import PartitionSpec as P

NLAT = 384
NLON = 1440
MODES = 384
ZL, YX, CH = 4, 16, 8
SLOTS = 6
ROWS, CHANS, FFN = 6, 32, 512
FULL = CH * CHANS
GROUPS, PAIR = 3, 2
PTS = 96
HALF = 90
LANES = 2 * PAIR * CHANS
BLOCK = 2 * ZL * PAIR
WIDE = YX * BLOCK
TILES = YX
BF = jnp.bfloat16
F32 = jnp.float32


def bf(a):
    return np.asarray(a, np.float32).astype(ml_dtypes.bfloat16)


@functools.lru_cache(None)
def constants():
    m, j = np.arange(MODES), np.arange(NLON)
    angle = 2 * np.pi * ((m[:, None] * j[None, :]) % NLON) / NLON
    waves = np.stack([np.cos(angle), -np.sin(angle)])
    fwd = bf((waves * (math.sqrt(2 * np.pi) / NLON)).reshape(2 * MODES, NLON))
    factor = np.where(m == 0, 1.0, 2.0) / math.sqrt(2 * np.pi)
    inv = (waves * factor[None, :, None]).reshape(2, MODES, CH, 2, HALF)
    inv = inv.transpose(3, 2, 4, 0, 1)
    inv = np.pad(inv, ((0, 0), (0, 0), (0, PTS - HALF), (0, 0), (0, 0)))
    inv = bf(inv.reshape(2, CH * PTS, 2 * MODES))
    spread = np.zeros((2, CH, PTS, NLON), np.float32)
    for half in range(2):
        for c in range(CH):
            for t in range(HALF):
                spread[half, c, t, 180 * c + HALF * half + t] = 1
    spread = bf(spread.reshape(2, CH * PTS, NLON))
    perm = np.zeros((WIDE, WIDE), np.float32)
    yx, p, zl, r = np.meshgrid(
        np.arange(YX), np.arange(2), np.arange(ZL), np.arange(PAIR), indexing="ij"
    )
    target = ((yx * 2 + p) * ZL + zl) * PAIR + r
    source = ((p * PAIR + r) * ZL + zl) * YX + yx
    perm[target.ravel(), source.ravel()] = 1
    slots = np.arange(MODES).reshape(ZL, YX, SLOTS).transpose(0, 2, 1).ravel()
    shuffle = np.zeros((MODES, MODES), np.float32)
    shuffle[np.arange(MODES), slots] = 1
    first = (zl * YX + yx) * ROWS + r
    row = np.concatenate([(first + PAIR * g).ravel() for g in range(GROUPS)])
    part = np.tile(p.ravel(), GROUPS)
    theta_all = (np.arange(NLAT) + 0.5) * np.pi / NLAT
    h = np.arange(1, NLAT // 2 + 1)
    series = np.cos(2 * theta_all[:, None] * h) / (4.0 * h * h - 1)
    quad_all = 2.0 / NLAT * (1 - 2 * series.sum(1))
    theta = theta_all[row]
    q = np.arange(1, MODES)
    aux = np.zeros((32, GROUPS * WIDE), np.float32)
    aux[0:6, :128] = np.cos(theta).reshape(6, 128)
    aux[8:14, :128] = np.log(np.sin(theta)).reshape(6, 128)
    aux[16] = quad_all[row] * (part == 0)
    aux[17] = quad_all[row] * (part == 1)
    aux[24, 1:MODES] = np.cumsum(0.5 * np.log((2.0 * q + 1) / (2.0 * q)))
    return fwd, inv, spread, bf(perm), bf(perm.T), bf(shuffle), aux


def dot(a, b, ca=1, cb=0):
    return lax.dot_general(a, b, (((ca,), (cb,)), ((), ())), preferred_element_type=F32)


def layer(
    ord_v, mask, x_h, aux_h, fwd_h, shuffle_h, perm_h, permt_h, spread_h, inv_h, w_h, inner_h, outer_h,
    out,
    x, aux, fwd, shuffle, perm, permt, spread, inv, wk, wa, wb, inner, outer, turned_mask,
    s1, r1, tmp, s2, r2, mix, s3, r3, s4, r4, ym, xt, s5, r5,
    acoef, ucoef, table, weighted, plain_t,
    lsem, wsend, wrecv, asend, arecv, bsend, brecv,
    s1s, s1r, s2s, s2r, s3s, s3r, s4s, s4r, s5s, s5r,
):
    lat, ch = lax.axis_index("lat"), lax.axis_index("chan")
    zl, yx = lat // YX, lax.rem(lat, YX)
    active = lax.rem(ch, 4) != 3
    slot = ch - ch // 4
    me_z = zl * CH + ch
    me_slot = zl * SLOTS + slot

    def chan_of(s):
        return s + s // 3

    def z_peer(i):
        return (i // CH) * YX + yx, lax.rem(i, CH)

    def z_holder(i):
        return (i // SLOTS) * YX + yx, chan_of(lax.rem(i, SLOTS))

    def z_far_first(i):
        t, core = i // 2, lax.rem(i, 2)
        away = 8 + (t + 1) // 2 * (1 - 2 * lax.rem(t, 2))
        z = lax.rem(ch // 2 * ZL + zl + away, 16)
        return lax.rem(z, ZL) * YX + yx, z // ZL * 2 + core

    def xy_peer(i):
        return zl * YX + i, ch

    def chan_peer(i):
        return lat, i

    def chan_holder(i):
        return lat, chan_of(i)

    def send(n, start, peer, src, dst, ssem, rsem):
        def body(i, carry):
            t = lax.rem(i + start, n)
            to = peer(t)
            mine = (to[0] == lat) & (to[1] == ch)

            @pl.when(jnp.logical_not(mine))
            def _():
                pltpu.make_async_remote_copy(
                    src_ref=src(t), dst_ref=dst, send_sem=ssem, recv_sem=rsem,
                    device_id=to, device_id_type=pl.DeviceIdType.MESH,
                ).start()

            @pl.when(mine)
            def _():
                pltpu.make_async_copy(src(t), dst, rsem).start()

            return carry

        lax.fori_loop(0, n, body, 0)

    def wait(ref, sem):
        pltpu.make_async_copy(ref, ref, sem).wait()

    loads = [
        pltpu.make_async_copy(a, b, lsem.at[k])
        for k, (a, b) in enumerate(
            (
                (x_h, x), (fwd_h, fwd), (shuffle_h, shuffle), (aux_h, aux), (spread_h, spread),
                (perm_h, perm), (permt_h, permt), (inv_h, inv),
            )
        )
    ]
    for load in loads[:4]:
        load.start()

    barrier = pltpu.get_barrier_semaphore()

    def greet(n, peer):
        def body(i, carry):
            to = peer(i)

            @pl.when((to[0] != lat) | (to[1] != ch))
            def _():
                pl.semaphore_signal(
                    barrier, inc=1, device_id=to, device_id_type=pl.DeviceIdType.MESH
                )

            return carry

        lax.fori_loop(0, n, body, 0)

    greet(ZL * CH, z_far_first)
    greet(YX, xy_peer)
    for load in loads[4:]:
        load.start()

    natural = lax.broadcasted_iota(jnp.int32, (MODES, MODES), 0)
    orders = ord_v[...].reshape(1, MODES)
    one_hot = jnp.where(natural == orders, 1.0, 0.0).astype(BF)
    loads[2].wait()
    select = dot(shuffle[...], one_hot, 1, 1).astype(BF)
    loads[0].wait()
    loads[1].wait()
    parts = [dot(fwd[k * MODES : (k + 1) * MODES, :], x[...], 1, 1) for k in range(2)]
    wide = PAIR * CHANS
    coeffs = jnp.concatenate(
        [parts[p][:, g * wide : (g + 1) * wide] for g in range(GROUPS) for p in range(2)], axis=1
    ).astype(BF)
    chosen = dot(select, coeffs).astype(BF)
    for g in range(GROUPS):
        lanes = slice(g * LANES, (g + 1) * LANES)
        s1[g] = chosen[:, lanes].reshape(ZL * SLOTS, YX, LANES)

    pl.semaphore_wait(barrier, ZL * CH - 1 + YX - 1)

    def send_mixing(p):
        send(SLOTS, lax.rem(ch, SLOTS), chan_holder,
             lambda t: w_h.at[t, p], wk.at[p, ch], wsend.at[p], wrecv.at[p])

    for g in range(GROUPS):
        send(ZL * SLOTS, zl * SLOTS + lax.rem(ch, SLOTS), z_holder,
             lambda t: s1.at[g, t], r1.at[g, me_z], s1s.at[g], s1r.at[g])
    tile_row = pl.multiple_of(lax.rem(yx // 2, 4) * 16, 16)
    tile_lane = pl.multiple_of(lax.rem(yx, 2) * 128, 128)

    @pl.when(yx < TILES // 2)
    def _():
        send(CH, ch, chan_peer, lambda t: inner_h.at[pl.ds(tile_row, 16), pl.ds(tile_lane, 128)],
             wa.at[ch], asend, arecv)

    @pl.when(yx >= TILES // 2)
    def _():
        send(CH, ch, chan_peer, lambda t: outer_h.at[pl.ds(tile_row, 16), pl.ds(tile_lane, 128)],
             wa.at[ch], asend, arecv)


    loads[4].wait()
    moved = [dot(spread[half], x[...], 1, 1) for half in range(2)]
    for g in range(GROUPS):
        xt[g] = jnp.concatenate(
            [moved[half][:, g * wide : (g + 1) * wide] for half in range(2)], axis=1
        ).astype(BF)
    loads[3].wait()
    padded = jnp.concatenate([mask[...].astype(F32), jnp.zeros((ROWS, 76), F32)], axis=1)
    padded = jnp.concatenate([padded, jnp.zeros((8 - ROWS, 256), F32)], axis=0)
    turned_mask[...] = padded.T

    @pl.when(active)
    def _():
        held = lax.broadcasted_iota(jnp.int32, (1, MODES), 1) == lat * SLOTS + slot
        order = jnp.sum(jnp.where(held, orders.astype(F32), 0.0), axis=1, keepdims=True)
        i = lax.broadcasted_iota(jnp.int32, (MODES, 128), 0).astype(F32)
        later = i >= 1.0
        degree = order + i
        low = i - 1.0
        prev = degree - 1.0
        a = jnp.sqrt(
            (4.0 * degree * degree - 1.0) / jnp.where(later, i * (2.0 * order + i), 1.0)
        )
        b = jnp.sqrt(
            jnp.maximum(low * (2.0 * order + low), 0.0)
            / jnp.maximum(4.0 * prev * prev - 1.0, 1.0)
        )
        acoef[...] = jnp.where(later, a, 0.0)
        ucoef[...] = jnp.where(later, a * b, 1.0)
        m_of = lax.broadcasted_iota(jnp.int32, (1, MODES), 1).astype(F32)
        picked = jnp.sum(
            jnp.where(m_of == order, aux[24:25, :MODES], 0.0), axis=1, keepdims=True
        )
        cosine = aux[0:8, :128]
        log_first = order * aux[8:16, :128] + (picked + 0.5 * math.log(0.5))

        def steps(t, carry):
            one, two, log_now = carry
            factor = jnp.exp(log_now)
            for s in range(8):
                k = t * 8 + s
                now = acoef[pl.ds(k, 1), :] * cosine * one - ucoef[pl.ds(k, 1), :] * two
                table[pl.ds(pl.multiple_of(k * 8, 8), 8), :] = now * factor
                one, two = now, one
            big = jnp.maximum(jnp.abs(one), jnp.abs(two)) > 2.0**40
            shrink = jnp.where(big, 2.0**-40, 1.0)
            log_now = log_now + jnp.where(big, 40.0 * math.log(2.0), 0.0)
            return one * shrink, two * shrink, log_now

        lax.fori_loop(
            0, MODES // 8, steps,
            (jnp.zeros((8, 128), F32), jnp.full((8, 128), -1.0, F32), log_first),
        )
        valid = i < MODES - order
        for k in range(GROUPS * WIDE // 128):
            lanes = slice(k * 128, (k + 1) * 128)
            part = jnp.where(valid, table[pl.ds(k, MODES, stride=8), :], 0.0)
            for p in range(2):
                weighted[p, :, lanes] = (part * aux[16 + p : 17 + p, lanes]).astype(BF)
            turned = part.T
            row = lax.broadcasted_iota(jnp.int32, (128, MODES), 0)
            which = lax.rem(row // (BLOCK // 2), 2)
            for p in range(2):
                plain_t[lanes, p * MODES : (p + 1) * MODES] = jnp.where(
                    which == p, turned, 0.0
                ).astype(BF)

    loads[5].wait()
    loads[6].wait()
    for g in range(GROUPS):

        @pl.when(active)
        def _():
            wait(s1.at[g, pl.ds(0, ZL * SLOTS - 1)], s1s.at[g])

        @pl.when(jnp.logical_not(active))
        def _():
            wait(s1.at[g], s1s.at[g])

    send_mixing(0)
    send_mixing(1)

    @pl.when(active)
    def _():
        for g in range(GROUPS):
            wait(r1.at[g], s1r.at[g])
            blocks = [
                jnp.concatenate([r1[g, z * CH + c] for z in range(ZL)], axis=0)
                for c in range(CH)
            ]
            for k in range(2 * PAIR):
                tmp[k * ZL * YX : (k + 1) * ZL * YX, :] = jnp.concatenate(
                    [blocks[c][:, k * CHANS : (k + 1) * CHANS] for c in range(CH)], axis=1
                )
            s2[g] = dot(perm[...], tmp[...]).astype(BF).reshape(YX, BLOCK, FULL)
            send(YX, yx, xy_peer, lambda t: s2.at[g, t], r2.at[g, yx], s2s.at[g], s2r.at[g])


    @pl.when(active)
    def _():
        spectra = [0.0, 0.0]
        for g in range(GROUPS):
            wait(r2.at[g], s2r.at[g])
            field = r2[g].reshape(WIDE, FULL)
            for p in range(2):
                spectra[p] += dot(weighted[p, :, g * WIDE : (g + 1) * WIDE], field)
        real, imag = (v.astype(BF) for v in spectra)
        for p in range(2):
            wait(wk.at[p], wrecv.at[p])
        w_real = wk[0].reshape(FULL, FULL)
        w_imag = wk[1].reshape(FULL, FULL)
        mix[0:MODES, :] = (dot(real, w_real, 1, 1) - dot(imag, w_imag, 1, 1)).astype(BF)
        mix[MODES:, :] = (dot(real, w_imag, 1, 1) + dot(imag, w_real, 1, 1)).astype(BF)
        for g in range(GROUPS):
            rows = slice(g * WIDE, (g + 1) * WIDE)
            s3[g] = dot(plain_t[rows, :], mix[...]).astype(BF).reshape(YX, BLOCK, FULL)
            send(YX, yx, xy_peer, lambda t: s3.at[g, t], r3.at[g, yx], s3s.at[g], s3r.at[g])
        for g in range(GROUPS):
            wait(r3.at[g], s3r.at[g])
            back = dot(permt[...], r3[g].reshape(WIDE, FULL)).astype(BF)
            for c in range(CH):
                piece = jnp.concatenate(
                    [
                        back[k * ZL * YX : (k + 1) * ZL * YX, c * CHANS : (c + 1) * CHANS]
                        for k in range(2 * PAIR)
                    ],
                    axis=1,
                )
                for z in range(ZL):
                    s4[g, z * CH + c] = piece[z * YX : (z + 1) * YX, :]
            send(ZL * CH, me_z, z_peer,
                 lambda t: s4.at[g, t], r4.at[g, me_slot], s4s.at[g], s4r.at[g])

    wait(wa, arecv)
    send(YX, yx, xy_peer, lambda t: wa, wb.at[yx], bsend, brecv)

    unselect = dot(one_hot, shuffle[...], 1, 1).astype(BF)
    loads[7].wait()
    for g in range(GROUPS):
        wait(r4.at[g], s4r.at[g])
        held = dot(unselect, r4[g].reshape(MODES, LANES)).astype(BF)
        ym[0:MODES, :] = held[:, :wide]
        ym[MODES:, :] = held[:, wide:]
        both = jnp.concatenate([dot(inv[half], ym[...]) for half in range(2)], axis=1)
        s5[g] = (both + xt[g].astype(F32)).astype(BF).reshape(CH, PTS, LANES)
        send(CH, ch, chan_peer, lambda t: s5.at[g, t], r5.at[g, ch], s5s.at[g], s5r.at[g])

    wait(wb, brecv)
    for t in range(TILES):
        whole = inner if t < TILES // 2 else outer
        a, b = (t // 2) % 4 * 16, t % 2 * 128
        whole[:, a : a + 16, b : b + 128] = wb[t]
    inner_all = inner[...].reshape(FFN, FULL)
    outer_all = outer[...].reshape(FFN, FULL)
    for g in range(GROUPS):
        wait(r5.at[g], s5r.at[g])
        hidden = jnp.concatenate(
            [
                jnp.concatenate(
                    [r5[g, c, :, k * CHANS : (k + 1) * CHANS] for c in range(CH)], axis=1
                )
                for k in range(2 * PAIR)
            ],
            axis=0,
        )
        activated = jax.nn.gelu(dot(hidden, inner_all, 1, 1)).astype(BF)
        total = hidden.astype(F32) + dot(activated, outer_all)
        for r in range(PAIR):
            row = PAIR * g + r
            points = jnp.concatenate(
                [
                    total[(half * PAIR + r) * PTS : (half * PAIR + r) * PTS + HALF, :]
                    for half in range(2)
                ],
                axis=0,
            )
            out[row] = (points * turned_mask[0 : 2 * HALF, row : row + 1]).astype(BF)

    for p in range(2):
        others = w_h.at[pl.ds(0, SLOTS - 1), p]

        @pl.when(active)
        def _():
            wait(others, wsend.at[p])

        @pl.when(jnp.logical_not(active))
        def _():
            wait(w_h.at[:, p], wsend.at[p])

    wait(wa.at[pl.ds(0, CH - 1)], asend)
    wait(wb.at[pl.ds(0, YX - 1)], bsend)
    for g in range(GROUPS):
        wait(s5.at[g, pl.ds(0, CH - 1)], s5s.at[g])

        @pl.when(active)
        def _():
            wait(s2.at[g, pl.ds(0, YX - 1)], s2s.at[g])
            wait(s3.at[g, pl.ds(0, YX - 1)], s3s.at[g])
            wait(s4.at[g, pl.ds(0, ZL * CH - 1)], s4s.at[g])


def local(ocean_state, land_mask, order_table, spectral_weight, inner_weight, outer_weight):
    fwd, inv, spread, perm, permt, shuffle, aux = constants()
    flat_state = ocean_state.reshape(ROWS * CHANS, NLON)
    vmem = pl.BlockSpec(memory_space=pltpu.VMEM)
    anywhere = pl.BlockSpec(memory_space=pl.ANY)
    sem = pltpu.SemaphoreType.DMA
    z_out, z_in = (ZL * SLOTS, YX, LANES), (ZL * CH, YX, LANES)

    def held(*shape):
        return pltpu.VMEM(shape, BF)

    return pl.pallas_call(
        layer,
        out_shape=jax.ShapeDtypeStruct((ROWS, 2 * HALF, FULL), BF),
        in_specs=[vmem] * 2 + [anywhere] * 11,
        out_specs=vmem,
        scratch_shapes=[
            held(*flat_state.shape),
            pltpu.VMEM(aux.shape, F32),
            held(*fwd.shape),
            held(*shuffle.shape),
            held(*perm.shape),
            held(*perm.shape),
            held(*spread.shape),
            held(*inv.shape),
            held(2, CH, CHANS, FULL),
            held(CH, 16, 128),
            held(YX, CH, 16, 128),
            held(CH, FFN // CH, FULL),
            held(CH, FFN // CH, FULL),
            pltpu.VMEM((256, 8), F32),
            held(GROUPS, *z_out),
            held(GROUPS, *z_in),
            held(WIDE, FULL),
            held(GROUPS, YX, BLOCK, FULL),
            held(GROUPS, YX, BLOCK, FULL),
            held(2 * MODES, FULL),
            held(GROUPS, YX, BLOCK, FULL),
            held(GROUPS, YX, BLOCK, FULL),
            held(GROUPS, *z_in),
            held(GROUPS, *z_out),
            held(2 * MODES, LANES // 2),
            held(GROUPS, CH * PTS, LANES),
            held(GROUPS, CH, PTS, LANES),
            held(GROUPS, CH, PTS, LANES),
            pltpu.VMEM((MODES, 128), F32),
            pltpu.VMEM((MODES, 128), F32),
            pltpu.VMEM((MODES * 8, 128), F32),
            held(2, MODES, GROUPS * WIDE),
            held(GROUPS * WIDE, 2 * MODES),
            sem((8,)),
            sem((2,)),
            sem((2,)),
            sem,
            sem,
            sem,
            sem,
        ]
        + [sem((GROUPS,))] * 10,
        compiler_params=pltpu.CompilerParams(
            collective_id=0, has_side_effects=True, vmem_limit_bytes=60 * 2**20
        ),
        cost_estimate=pl.CostEstimate(
            flops=2 * 10**9, bytes_accessed=12 * 10**6, transcendentals=10**5
        ),
    )(
        order_table, land_mask, flat_state, aux, fwd, shuffle, perm, permt, spread, inv,
        spectral_weight, inner_weight.T, outer_weight,
    )


def solution(mesh):
    placed = (
        P("lat", "chan", None),
        P("lat", "chan"),
        P(),
        P("lat", None, "chan", None),
        P(None, "chan"),
        P("chan", None),
    )
    return jax.shard_map(
        local, mesh=mesh, in_specs=placed, out_specs=P("lat", "chan", None), check_vma=False
    )
```

```python
import functools
import math

import jax
import jax.numpy as jnp
import ml_dtypes
import numpy as np
from jax import lax
from jax.experimental import pallas as pl
from jax.experimental.pallas import tpu as pltpu
from jax.sharding import PartitionSpec as P

NLAT = 384
NLON = 1440
MODES = 384
ZL, YX, CH = 4, 16, 8
SLOTS = 6
ROWS, CHANS, FFN = 6, 32, 512
FULL = CH * CHANS
GROUPS, PAIR = 3, 2
PTS = 96
HALF = 90
LANES = 2 * PAIR * CHANS
BLOCK = 2 * ZL * PAIR
WIDE = YX * BLOCK
TILES = YX
BF = jnp.bfloat16
F32 = jnp.float32


def bf(a):
    return np.asarray(a, np.float32).astype(ml_dtypes.bfloat16)


@functools.lru_cache(None)
def constants():
    m, j = np.arange(MODES), np.arange(NLON)
    angle = 2 * np.pi * ((m[:, None] * j[None, :]) % NLON) / NLON
    waves = np.stack([np.cos(angle), -np.sin(angle)])
    fwd = bf((waves * (math.sqrt(2 * np.pi) / NLON)).reshape(2 * MODES, NLON))
    factor = np.where(m == 0, 1.0, 2.0) / math.sqrt(2 * np.pi)
    inv = (waves * factor[None, :, None]).reshape(2, MODES, CH, 2, HALF)
    inv = inv.transpose(3, 2, 4, 0, 1)
    inv = np.pad(inv, ((0, 0), (0, 0), (0, PTS - HALF), (0, 0), (0, 0)))
    inv = bf(inv.reshape(2, CH * PTS, 2 * MODES))
    spread = np.zeros((2, CH, PTS, NLON), np.float32)
    for half in range(2):
        for c in range(CH):
            for t in range(HALF):
                spread[half, c, t, 180 * c + HALF * half + t] = 1
    spread = bf(spread.reshape(2, CH * PTS, NLON))
    perm = np.zeros((WIDE, WIDE), np.float32)
    yx, p, zl, r = np.meshgrid(
        np.arange(YX), np.arange(2), np.arange(ZL), np.arange(PAIR), indexing="ij"
    )
    target = ((yx * 2 + p) * ZL + zl) * PAIR + r
    source = ((p * PAIR + r) * ZL + zl) * YX + yx
    perm[target.ravel(), source.ravel()] = 1
    slots = np.arange(MODES).reshape(ZL, YX, SLOTS).transpose(0, 2, 1).ravel()
    shuffle = np.zeros((MODES, MODES), np.float32)
    shuffle[np.arange(MODES), slots] = 1
    first = (zl * YX + yx) * ROWS + r
    row = np.concatenate([(first + PAIR * g).ravel() for g in range(GROUPS)])
    part = np.tile(p.ravel(), GROUPS)
    theta_all = (np.arange(NLAT) + 0.5) * np.pi / NLAT
    h = np.arange(1, NLAT // 2 + 1)
    series = np.cos(2 * theta_all[:, None] * h) / (4.0 * h * h - 1)
    quad_all = 2.0 / NLAT * (1 - 2 * series.sum(1))
    theta = theta_all[row]
    q = np.arange(1, MODES)
    aux = np.zeros((32, GROUPS * WIDE), np.float32)
    aux[0:6, :128] = np.cos(theta).reshape(6, 128)
    aux[8:14, :128] = np.log(np.sin(theta)).reshape(6, 128)
    aux[16] = quad_all[row] * (part == 0)
    aux[17] = quad_all[row] * (part == 1)
    aux[24, 1:MODES] = np.cumsum(0.5 * np.log((2.0 * q + 1) / (2.0 * q)))
    return fwd, inv, spread, bf(perm), bf(perm.T), bf(shuffle), aux


def dot(a, b, ca=1, cb=0):
    return lax.dot_general(a, b, (((ca,), (cb,)), ((), ())), preferred_element_type=F32)


def layer(
    ord_v, mask, x_h, aux_h, fwd_h, shuffle_h, perm_h, permt_h, spread_h, inv_h, w_h, inner_h, outer_h,
    out,
    x, aux, fwd, shuffle, perm, permt, spread, inv, wk, wa, wb, inner, outer, turned_mask,
    s1, r1, tmp, s2, r2, mix, s3, r3, s4, r4, ym, xt, s5, r5,
    acoef, ucoef, table, weighted, plain_t,
    lsem, wsend, wrecv, asend, arecv, bsend, brecv,
    s1s, s1r, s2s, s2r, s3s, s3r, s4s, s4r, s5s, s5r,
):
    lat, ch = lax.axis_index("lat"), lax.axis_index("chan")
    zl, yx = lat // YX, lax.rem(lat, YX)
    odd = lax.rem(zl, 2)
    active = lax.rem(ch, 4) != 3 - 2 * odd
    slot = ch - (ch + 2 * odd) // 4
    me_z = zl * CH + ch
    me_slot = zl * SLOTS + slot

    def chan_of(s, z):
        return s + (s + 2 * lax.rem(z, 2)) // 3

    def z_peer(i):
        return (i // CH) * YX + yx, lax.rem(i, CH)

    def z_holder(i):
        return (i // SLOTS) * YX + yx, chan_of(lax.rem(i, SLOTS), i // SLOTS)

    def z_far_first(i):
        t, core = i // 2, lax.rem(i, 2)
        away = 8 + (t + 1) // 2 * (1 - 2 * lax.rem(t, 2))
        z = lax.rem(ch // 2 * ZL + zl + away, 16)
        return lax.rem(z, ZL) * YX + yx, z // ZL * 2 + core

    def xy_peer(i):
        return zl * YX + i, ch

    def chan_peer(i):
        return lat, i

    def chan_holder(i):
        return lat, chan_of(i, zl)

    def send(n, start, peer, src, dst, ssem, rsem):
        def body(i, carry):
            t = lax.rem(i + start, n)
            to = peer(t)
            mine = (to[0] == lat) & (to[1] == ch)

            @pl.when(jnp.logical_not(mine))
            def _():
                pltpu.make_async_remote_copy(
                    src_ref=src(t), dst_ref=dst, send_sem=ssem, recv_sem=rsem,
                    device_id=to, device_id_type=pl.DeviceIdType.MESH,
                ).start()

            @pl.when(mine)
            def _():
                pltpu.make_async_copy(src(t), dst, rsem).start()

            return carry

        lax.fori_loop(0, n, body, 0)

    def wait(ref, sem):
        pltpu.make_async_copy(ref, ref, sem).wait()

    loads = [
        pltpu.make_async_copy(a, b, lsem.at[k])
        for k, (a, b) in enumerate(
            (
                (x_h, x), (fwd_h, fwd), (shuffle_h, shuffle), (aux_h, aux), (spread_h, spread),
                (perm_h, perm), (permt_h, permt), (inv_h, inv),
            )
        )
    ]
    for load in loads[:4]:
        load.start()

    barrier = pltpu.get_barrier_semaphore()

    def greet(n, peer):
        def body(i, carry):
            to = peer(i)

            @pl.when((to[0] != lat) | (to[1] != ch))
            def _():
                pl.semaphore_signal(
                    barrier, inc=1, device_id=to, device_id_type=pl.DeviceIdType.MESH
                )

            return carry

        lax.fori_loop(0, n, body, 0)

    greet(ZL * CH, z_far_first)
    greet(YX, xy_peer)
    for load in loads[4:]:
        load.start()

    natural = lax.broadcasted_iota(jnp.int32, (MODES, MODES), 0)
    orders = ord_v[...].reshape(1, MODES)
    one_hot = jnp.where(natural == orders, 1.0, 0.0).astype(BF)
    loads[2].wait()
    select = dot(shuffle[...], one_hot, 1, 1).astype(BF)
    loads[0].wait()
    loads[1].wait()
    parts = [dot(fwd[k * MODES : (k + 1) * MODES, :], x[...], 1, 1) for k in range(2)]
    wide = PAIR * CHANS
    coeffs = jnp.concatenate(
        [parts[p][:, g * wide : (g + 1) * wide] for g in range(GROUPS) for p in range(2)], axis=1
    ).astype(BF)
    chosen = dot(select, coeffs).astype(BF)
    for g in range(GROUPS):
        lanes = slice(g * LANES, (g + 1) * LANES)
        s1[g] = chosen[:, lanes].reshape(ZL * SLOTS, YX, LANES)

    pl.semaphore_wait(barrier, ZL * CH - 1 + YX - 1)

    def send_mixing(p):
        send(SLOTS, lax.rem(ch, SLOTS), chan_holder,
             lambda t: w_h.at[t, p], wk.at[p, ch], wsend.at[p], wrecv.at[p])

    for g in range(GROUPS):
        send(ZL * SLOTS, zl * SLOTS + lax.rem(ch, SLOTS), z_holder,
             lambda t: s1.at[g, t], r1.at[g, me_z], s1s.at[g], s1r.at[g])
    tile_row = pl.multiple_of(lax.rem(yx // 2, 4) * 16, 16)
    tile_lane = pl.multiple_of(lax.rem(yx, 2) * 128, 128)

    @pl.when(yx < TILES // 2)
    def _():
        send(CH, ch, chan_peer, lambda t: inner_h.at[pl.ds(tile_row, 16), pl.ds(tile_lane, 128)],
             wa.at[ch], asend, arecv)

    @pl.when(yx >= TILES // 2)
    def _():
        send(CH, ch, chan_peer, lambda t: outer_h.at[pl.ds(tile_row, 16), pl.ds(tile_lane, 128)],
             wa.at[ch], asend, arecv)


    loads[4].wait()
    moved = [dot(spread[half], x[...], 1, 1) for half in range(2)]
    for g in range(GROUPS):
        xt[g] = jnp.concatenate(
            [moved[half][:, g * wide : (g + 1) * wide] for half in range(2)], axis=1
        ).astype(BF)
    loads[3].wait()
    padded = jnp.concatenate([mask[...].astype(F32), jnp.zeros((ROWS, 76), F32)], axis=1)
    padded = jnp.concatenate([padded, jnp.zeros((8 - ROWS, 256), F32)], axis=0)
    turned_mask[...] = padded.T

    @pl.when(active)
    def _():
        held = lax.broadcasted_iota(jnp.int32, (1, MODES), 1) == lat * SLOTS + slot
        order = jnp.sum(jnp.where(held, orders.astype(F32), 0.0), axis=1, keepdims=True)
        i = lax.broadcasted_iota(jnp.int32, (MODES, 128), 0).astype(F32)
        later = i >= 1.0
        degree = order + i
        low = i - 1.0
        prev = degree - 1.0
        a = jnp.sqrt(
            (4.0 * degree * degree - 1.0) / jnp.where(later, i * (2.0 * order + i), 1.0)
        )
        b = jnp.sqrt(
            jnp.maximum(low * (2.0 * order + low), 0.0)
            / jnp.maximum(4.0 * prev * prev - 1.0, 1.0)
        )
        acoef[...] = jnp.where(later, a, 0.0)
        ucoef[...] = jnp.where(later, a * b, 1.0)
        m_of = lax.broadcasted_iota(jnp.int32, (1, MODES), 1).astype(F32)
        picked = jnp.sum(
            jnp.where(m_of == order, aux[24:25, :MODES], 0.0), axis=1, keepdims=True
        )
        cosine = aux[0:8, :128]
        log_first = order * aux[8:16, :128] + (picked + 0.5 * math.log(0.5))

        def steps(t, carry):
            one, two, log_now = carry
            factor = jnp.exp(log_now)
            for s in range(8):
                k = t * 8 + s
                now = acoef[pl.ds(k, 1), :] * cosine * one - ucoef[pl.ds(k, 1), :] * two
                table[pl.ds(pl.multiple_of(k * 8, 8), 8), :] = now * factor
                one, two = now, one
            big = jnp.maximum(jnp.abs(one), jnp.abs(two)) > 2.0**40
            shrink = jnp.where(big, 2.0**-40, 1.0)
            log_now = log_now + jnp.where(big, 40.0 * math.log(2.0), 0.0)
            return one * shrink, two * shrink, log_now

        lax.fori_loop(
            0, MODES // 8, steps,
            (jnp.zeros((8, 128), F32), jnp.full((8, 128), -1.0, F32), log_first),
        )
        valid = i < MODES - order
        for k in range(GROUPS * WIDE // 128):
            lanes = slice(k * 128, (k + 1) * 128)
            part = jnp.where(valid, table[pl.ds(k, MODES, stride=8), :], 0.0)
            for p in range(2):
                weighted[p, :, lanes] = (part * aux[16 + p : 17 + p, lanes]).astype(BF)
            turned = part.T
            row = lax.broadcasted_iota(jnp.int32, (128, MODES), 0)
            which = lax.rem(row // (BLOCK // 2), 2)
            for p in range(2):
                plain_t[lanes, p * MODES : (p + 1) * MODES] = jnp.where(
                    which == p, turned, 0.0
                ).astype(BF)

    loads[5].wait()
    loads[6].wait()
    for g in range(GROUPS):

        @pl.when(active)
        def _():
            wait(s1.at[g, pl.ds(0, ZL * SLOTS - 1)], s1s.at[g])

        @pl.when(jnp.logical_not(active))
        def _():
            wait(s1.at[g], s1s.at[g])

    send_mixing(0)
    send_mixing(1)

    @pl.when(active)
    def _():
        for g in range(GROUPS):
            wait(r1.at[g], s1r.at[g])
            blocks = [
                jnp.concatenate([r1[g, z * CH + c] for z in range(ZL)], axis=0)
                for c in range(CH)
            ]
            for k in range(2 * PAIR):
                tmp[k * ZL * YX : (k + 1) * ZL * YX, :] = jnp.concatenate(
                    [blocks[c][:, k * CHANS : (k + 1) * CHANS] for c in range(CH)], axis=1
                )
            s2[g] = dot(perm[...], tmp[...]).astype(BF).reshape(YX, BLOCK, FULL)
            send(YX, yx, xy_peer, lambda t: s2.at[g, t], r2.at[g, yx], s2s.at[g], s2r.at[g])


    @pl.when(active)
    def _():
        spectra = [0.0, 0.0]
        for g in range(GROUPS):
            wait(r2.at[g], s2r.at[g])
            field = r2[g].reshape(WIDE, FULL)
            for p in range(2):
                spectra[p] += dot(weighted[p, :, g * WIDE : (g + 1) * WIDE], field)
        real, imag = (v.astype(BF) for v in spectra)
        for p in range(2):
            wait(wk.at[p], wrecv.at[p])
        w_real = wk[0].reshape(FULL, FULL)
        w_imag = wk[1].reshape(FULL, FULL)
        mix[0:MODES, :] = (dot(real, w_real, 1, 1) - dot(imag, w_imag, 1, 1)).astype(BF)
        mix[MODES:, :] = (dot(real, w_imag, 1, 1) + dot(imag, w_real, 1, 1)).astype(BF)
        for g in range(GROUPS):
            rows = slice(g * WIDE, (g + 1) * WIDE)
            s3[g] = dot(plain_t[rows, :], mix[...]).astype(BF).reshape(YX, BLOCK, FULL)
            send(YX, yx, xy_peer, lambda t: s3.at[g, t], r3.at[g, yx], s3s.at[g], s3r.at[g])
        for g in range(GROUPS):
            wait(r3.at[g], s3r.at[g])
            back = dot(permt[...], r3[g].reshape(WIDE, FULL)).astype(BF)
            for c in range(CH):
                piece = jnp.concatenate(
                    [
                        back[k * ZL * YX : (k + 1) * ZL * YX, c * CHANS : (c + 1) * CHANS]
                        for k in range(2 * PAIR)
                    ],
                    axis=1,
                )
                for z in range(ZL):
                    s4[g, z * CH + c] = piece[z * YX : (z + 1) * YX, :]
            send(ZL * CH, me_z, z_peer,
                 lambda t: s4.at[g, t], r4.at[g, me_slot], s4s.at[g], s4r.at[g])

    unselect = dot(one_hot, shuffle[...], 1, 1).astype(BF)
    loads[7].wait()
    for g in range(GROUPS):
        wait(r4.at[g], s4r.at[g])
        if g == 0:
            wait(wa, arecv)
            send(YX, yx, xy_peer, lambda t: wa, wb.at[yx], bsend, brecv)
        held = dot(unselect, r4[g].reshape(MODES, LANES)).astype(BF)
        ym[0:MODES, :] = held[:, :wide]
        ym[MODES:, :] = held[:, wide:]
        both = jnp.concatenate([dot(inv[half], ym[...]) for half in range(2)], axis=1)
        s5[g] = (both + xt[g].astype(F32)).astype(BF).reshape(CH, PTS, LANES)
        send(CH, ch, chan_peer, lambda t: s5.at[g, t], r5.at[g, ch], s5s.at[g], s5r.at[g])

    wait(wb, brecv)
    for t in range(TILES):
        whole = inner if t < TILES // 2 else outer
        a, b = (t // 2) % 4 * 16, t % 2 * 128
        whole[:, a : a + 16, b : b + 128] = wb[t]
    inner_all = inner[...].reshape(FFN, FULL)
    outer_all = outer[...].reshape(FFN, FULL)
    for g in range(GROUPS):
        wait(r5.at[g], s5r.at[g])
        hidden = jnp.concatenate(
            [
                jnp.concatenate(
                    [r5[g, c, :, k * CHANS : (k + 1) * CHANS] for c in range(CH)], axis=1
                )
                for k in range(2 * PAIR)
            ],
            axis=0,
        )
        activated = jax.nn.gelu(dot(hidden, inner_all, 1, 1)).astype(BF)
        total = hidden.astype(F32) + dot(activated, outer_all)
        for r in range(PAIR):
            row = PAIR * g + r
            points = jnp.concatenate(
                [
                    total[(half * PAIR + r) * PTS : (half * PAIR + r) * PTS + HALF, :]
                    for half in range(2)
                ],
                axis=0,
            )
            out[row] = (points * turned_mask[0 : 2 * HALF, row : row + 1]).astype(BF)

    for p in range(2):
        others = w_h.at[pl.ds(0, SLOTS - 1), p]

        @pl.when(active)
        def _():
            wait(others, wsend.at[p])

        @pl.when(jnp.logical_not(active))
        def _():
            wait(w_h.at[:, p], wsend.at[p])

    wait(wa.at[pl.ds(0, CH - 1)], asend)
    wait(wb.at[pl.ds(0, YX - 1)], bsend)
    for g in range(GROUPS):
        wait(s5.at[g, pl.ds(0, CH - 1)], s5s.at[g])

        @pl.when(active)
        def _():
            wait(s2.at[g, pl.ds(0, YX - 1)], s2s.at[g])
            wait(s3.at[g, pl.ds(0, YX - 1)], s3s.at[g])
            wait(s4.at[g, pl.ds(0, ZL * CH - 1)], s4s.at[g])


def local(ocean_state, land_mask, order_table, spectral_weight, inner_weight, outer_weight):
    fwd, inv, spread, perm, permt, shuffle, aux = constants()
    flat_state = ocean_state.reshape(ROWS * CHANS, NLON)
    vmem = pl.BlockSpec(memory_space=pltpu.VMEM)
    anywhere = pl.BlockSpec(memory_space=pl.ANY)
    sem = pltpu.SemaphoreType.DMA
    z_out, z_in = (ZL * SLOTS, YX, LANES), (ZL * CH, YX, LANES)

    def held(*shape):
        return pltpu.VMEM(shape, BF)

    return pl.pallas_call(
        layer,
        out_shape=jax.ShapeDtypeStruct((ROWS, 2 * HALF, FULL), BF),
        in_specs=[vmem] * 2 + [anywhere] * 11,
        out_specs=vmem,
        scratch_shapes=[
            held(*flat_state.shape),
            pltpu.VMEM(aux.shape, F32),
            held(*fwd.shape),
            held(*shuffle.shape),
            held(*perm.shape),
            held(*perm.shape),
            held(*spread.shape),
            held(*inv.shape),
            held(2, CH, CHANS, FULL),
            held(CH, 16, 128),
            held(YX, CH, 16, 128),
            held(CH, FFN // CH, FULL),
            held(CH, FFN // CH, FULL),
            pltpu.VMEM((256, 8), F32),
            held(GROUPS, *z_out),
            held(GROUPS, *z_in),
            held(WIDE, FULL),
            held(GROUPS, YX, BLOCK, FULL),
            held(GROUPS, YX, BLOCK, FULL),
            held(2 * MODES, FULL),
            held(GROUPS, YX, BLOCK, FULL),
            held(GROUPS, YX, BLOCK, FULL),
            held(GROUPS, *z_in),
            held(GROUPS, *z_out),
            held(2 * MODES, LANES // 2),
            held(GROUPS, CH * PTS, LANES),
            held(GROUPS, CH, PTS, LANES),
            held(GROUPS, CH, PTS, LANES),
            pltpu.VMEM((MODES, 128), F32),
            pltpu.VMEM((MODES, 128), F32),
            pltpu.VMEM((MODES * 8, 128), F32),
            held(2, MODES, GROUPS * WIDE),
            held(GROUPS * WIDE, 2 * MODES),
            sem((8,)),
            sem((2,)),
            sem((2,)),
            sem,
            sem,
            sem,
            sem,
        ]
        + [sem((GROUPS,))] * 10,
        compiler_params=pltpu.CompilerParams(
            collective_id=0, has_side_effects=True, vmem_limit_bytes=60 * 2**20
        ),
        cost_estimate=pl.CostEstimate(
            flops=2 * 10**9, bytes_accessed=12 * 10**6, transcendentals=10**5
        ),
    )(
        order_table, land_mask, flat_state, aux, fwd, shuffle, perm, permt, spread, inv,
        spectral_weight, inner_weight.T, outer_weight,
    )


def solution(mesh):
    placed = (
        P("lat", "chan", None),
        P("lat", "chan"),
        P(),
        P("lat", None, "chan", None),
        P(None, "chan"),
        P("chan", None),
    )
    return jax.shard_map(
        local, mesh=mesh, in_specs=placed, out_specs=P("lat", "chan", None), check_vma=False
    )
```
